32 devices in a mesh: dp: 8 (over z, x), expert: 4 (over y, core).
Axes of the slice: x: 2, y: 2, z: 4, core: 2. Of those that a mesh axis runs over, the one named last changes fastest.
Arguments:
- tokens: bfloat16 [4096, 3584], P('dp'), may hold values from -6 to 6
- grad_out: bfloat16 [4096, 3584], P('dp'), may hold values from -6 to 6
- route_rows: int32 [4096], P('dp'), may hold values from 0 to 511, as said below
- route_gate: float32 [4096], P('dp'), may hold values from 0.1 to 1
- block_count: int32 [8], P('dp'), may hold values from 0 to 4, as said below
- gate_weight: bfloat16 [3584, 2048], P('dp', 'expert'), may hold values from -0.125 to 0.125
- up_weight: bfloat16 [3584, 2048], P('dp', 'expert'), may hold values from -0.125 to 0.125
- down_weight_t: bfloat16 [3584, 2048], P('dp', 'expert'), may hold values from -0.125 to 0.125
Outputs:
- grad_tokens: bfloat16 [4096, 3584], P('dp', 'expert')
- grad_gate_weight: float32 [3584, 2048], P('dp', 'expert')
- grad_up_weight: float32 [3584, 2048], P('dp', 'expert')
The draws below stay inside these ranges and needn't reach their ends.
Inputs may be any that keep to these rules, and one draw needn't show every extreme that they name: `route_rows`: each index of dp holds 512 entries that are a permutation of 0 to 511. Slots 0 to block_count * 128 - 1 of an index of dp are live, its other slots empty; some index has all 4 blocks live and some index none.
All inputs are finite; a program needn't handle non-finite values.
Results may differ from the reference program's by a relative error of at most 0.017.
Values may be sent and summed in bfloat16 or wider, within the bound.
A program may use at most 64 MiB of HBM per device.

```python
import math
import jax
import jax.numpy as jnp
from jax import lax

D = 3584
FF = 2048
T_DEV = 512
BLOCK = 128
NBLK = 4
HD = 512
TOKENS = 4096
N_DP = 8
N_EXPERT = 4


def draw_route_rows(key, part):
    device_keys = jax.random.split(jax.random.fold_in(key, 11), N_DP)
    orders = jax.vmap(lambda device_key: jax.random.permutation(device_key, T_DEV))(device_keys)
    return orders.reshape(-1).astype(jnp.int32)


def draw_block_count(key, part):
    levels = jax.random.randint(jax.random.fold_in(key, 21), (N_DP,), 0, 20)
    counts = jnp.where(levels < 4, 0, jnp.where(levels < 10, NBLK // 2, NBLK))
    chosen = jax.random.randint(jax.random.fold_in(key, 22), (), 0, N_DP)
    other_step = jax.random.randint(jax.random.fold_in(key, 23), (), 0, N_DP - 1)
    emptied = (chosen + 1 + other_step) % N_DP
    positions = jnp.arange(N_DP)
    counts = jnp.where(positions == chosen, NBLK, counts)
    counts = jnp.where(positions == emptied, 0, counts)
    return counts.astype(jnp.int32)


def strengthened(values, stream_key, source, target, blocks, factor):
    owner, partner = [(jnp.arange(values.shape[position]) // (values.shape[position] // blocks)).reshape([-1 if axis == position else 1 for axis in range(values.ndim)]) for position in (source, target)]
    chosen = jax.random.permutation(stream_key, blocks)[partner]
    strong = (owner == chosen) | (owner == (partner + blocks // 2) % blocks)
    return jnp.where(strong, factor * values, values)


def steps_of(own_key, dims, cuts, least, largest):
    def one(axis_at, shards_of):
        heights = jax.random.uniform(jax.random.fold_in(jax.random.fold_in(own_key, 6), axis_at), (shards_of,), jnp.float32, least / len(cuts), largest / len(cuts))
        return jnp.repeat(jnp.exp(heights), dims[axis_at] // shards_of).reshape((-1,) + (1,) * (len(dims) - axis_at - 1))

    level = one(*cuts[0])
    for cut in cuts[1:]:
        level = level * one(*cut)
    return level


def normal_values(own_key, shape, spread, reach, cuts=(), held_as=jnp.bfloat16):
    result = jax.random.normal(own_key, shape, jnp.float32) * spread
    if len(cuts) > 0:
        result = steps_of(own_key, shape, cuts, -0.22, 0.18) * result
    return jnp.clip(result, min=-reach, max=reach).astype(held_as)


def gaussian_with(stream_key, extent, deviation, limit, shards, heavy, dtype=jnp.bfloat16):
    result = deviation * jax.random.normal(stream_key, extent, jnp.float32)
    if shards:
        result = result * steps_of(stream_key, extent, shards, -0.22, 0.18)
    return jnp.clip(strengthened(result, jax.random.fold_in(stream_key, 3), *heavy), -limit, limit).astype(dtype)


def setup_inputs(seed: int = 0) -> dict:
    splits = jax.random.split(jax.random.key(seed), 9)
    tokens = gaussian_with(splits[0], (TOKENS, D), 1.0, 6.0, ((0, 8),), (0, 1, 8, 2.0))
    grad_out = normal_values(splits[1], (TOKENS, D), 1.0, 6.0, ((0, 8),))
    route_rows = draw_route_rows(jax.random.fold_in(splits[8], 71), 0)
    route_gate = jnp.clip(jnp.exp(math.log(1.0) - 2.3025851 * jax.random.uniform(splits[3], (TOKENS,), jnp.float32) ** steps_of(splits[3], (TOKENS,), ((0, 8),), -0.2, 0.2)), 0.1, 1.0)
    block_count = draw_block_count(jax.random.fold_in(splits[8], 71), 0)
    gate_weight = gaussian_with(splits[5], (D, FF), D ** -0.5, 0.125, ((0, 8), (1, 4)), (1, 0, 8, 2.0))
    up_weight = gaussian_with(splits[6], (D, FF), D ** -0.5, 0.125, ((0, 8), (1, 4)), (1, 0, 8, 2.0))
    down_weight_t = normal_values(splits[7], (D, FF), FF ** -0.5, 0.125, ((0, 8), (1, 4)))
    return {"tokens": tokens, "grad_out": grad_out, "route_rows": route_rows, "route_gate": route_gate, "block_count": block_count, "gate_weight": gate_weight, "up_weight": up_weight, "down_weight_t": down_weight_t}


def reference(tokens, grad_out, route_rows, route_gate, block_count, gate_weight, up_weight, down_weight_t):
    def device_pass(running, device_item):
        sum_gate, sum_up = running
        token_dev, cotangent_dev, rows_dev, gates_dev, live_count = device_item

        def block_step(block_index, state_inner):
            acc_gate, acc_up, input_dev = state_inner
            offset = block_index * BLOCK
            rows_block = lax.dynamic_slice_in_dim(rows_dev, offset, BLOCK, 0)
            token_block = jnp.take(token_dev, rows_block, axis=0)
            cotangent_block = jnp.take(cotangent_dev, rows_block, axis=0)
            weight_block = lax.dynamic_slice_in_dim(gates_dev, offset, BLOCK, 0)
            gate_val = jnp.dot(token_block, gate_weight, preferred_element_type=jnp.float32)
            up_val = jnp.dot(token_block, up_weight, preferred_element_type=jnp.float32)
            backward = jnp.dot(cotangent_block, down_weight_t, preferred_element_type=jnp.float32)
            hidden_grad = weight_block[:, None] * backward
            gate_sigmoid = jax.nn.sigmoid(gate_val)
            grad_up = (hidden_grad * (gate_val * gate_sigmoid)).astype(jnp.bfloat16)
            grad_gate = (hidden_grad * up_val * gate_sigmoid * (1.0 + gate_val * (1.0 - gate_sigmoid))).astype(jnp.bfloat16)
            summed_rows = jnp.zeros((BLOCK, D), jnp.float32)
            for column_group in range(N_EXPERT):
                lower_col = column_group * HD
                upper_col = lower_col + HD
                partial_sum = jnp.dot(grad_gate[:, lower_col:upper_col], gate_weight[:, lower_col:upper_col].T, preferred_element_type=jnp.float32)
                partial_sum = partial_sum + jnp.dot(grad_up[:, lower_col:upper_col], up_weight[:, lower_col:upper_col].T, preferred_element_type=jnp.float32)
                partial_sum = lax.optimization_barrier(partial_sum.astype(jnp.bfloat16))
                summed_rows = summed_rows + partial_sum.astype(jnp.float32)
            input_dev = input_dev.at[rows_block].set(summed_rows.astype(jnp.bfloat16))
            acc_gate = acc_gate + jnp.dot(token_block.T, grad_gate, preferred_element_type=jnp.float32)
            acc_up = acc_up + jnp.dot(token_block.T, grad_up, preferred_element_type=jnp.float32)
            return acc_gate, acc_up, input_dev

        start_state = (sum_gate, sum_up, jnp.zeros((T_DEV, D), jnp.bfloat16))
        sum_gate, sum_up, input_dev = lax.fori_loop(0, live_count, block_step, start_state)
        return (sum_gate, sum_up), input_dev

    zero_grad = jnp.zeros((D, FF), jnp.float32)
    device_items = (tokens.reshape(N_DP, T_DEV, D), grad_out.reshape(N_DP, T_DEV, D), route_rows.reshape(N_DP, T_DEV), route_gate.reshape(N_DP, T_DEV), block_count)
    (sum_gate, sum_up), inputs_all = lax.scan(device_pass, (zero_grad, zero_grad), device_items)
    grad_scale = float(TOKENS) ** -0.5
    return inputs_all.reshape(TOKENS, D), sum_gate * grad_scale, sum_up * grad_scale
```

```python
import functools

import jax
import jax.numpy as jnp
from jax import lax
from jax.experimental import pallas as pl
from jax.experimental.pallas import tpu as pltpu
from jax.sharding import PartitionSpec as P

BLOCK = 128
MESH = pl.DeviceIdType.MESH
Z, X, Y, C = 4, 2, 2, 2
HALVES = 2
PIECES = 3 * HALVES
X_FIRST = (0,)
RIGHT, LEFT, ACROSS = 0, 1, 2


def kernel(
    scale,
    tokens_hbm, cotangent_hbm, routes_ref, gates_ref, count_ref, gate_hbm, up_hbm, down_hbm,
    grad_tokens_ref, grad_gate_ref, grad_up_ref,
    tokens, cotangent, panel, flipped, gate_acc, up_acc, back_acc, grads, row_gate,
    own_sum, cross_out, cross_in, right_sum, left_sum, share_out, share_in,
    load_sem, gather_send, gather_recv, cross_send, cross_recv,
    line_send, line_recv, share_send, share_recv,
):
    dp, expert = lax.axis_index("dp"), lax.axis_index("expert")
    z, x = dp // X, dp % X
    y, c = expert // C, expert % C
    other_x = 1 - x
    weights = (gate_hbm, up_hbm, down_hbm)
    shard_rows, width = gate_hbm.shape
    piece_rows = shard_rows // HALVES
    pair_rows = X * shard_rows
    row_count = tokens.shape[0]

    across = (z * X + other_x, expert)
    targets = {RIGHT: (dp + X, expert), LEFT: (dp - X, expert), ACROSS: across}
    has = {RIGHT: z < Z - 1, LEFT: z > 0}

    def when(direction, fn):
        if direction == ACROSS:
            fn()
        else:
            pl.when(has[direction])(fn)

    share_targets = []
    for j in range(1, Y * C):
        y_to = 1 - y if j // C else y
        c_to = 1 - c if j % C else c
        share_targets.append(y_to * C + c_to)

    barrier = pltpu.get_barrier_semaphore()
    for direction in (RIGHT, LEFT, ACROSS):
        when(direction, lambda direction=direction: pl.semaphore_signal(
            barrier, inc=1, device_id=targets[direction], device_id_type=MESH))
    for to in share_targets:
        pl.semaphore_signal(barrier, inc=1, device_id=(dp, to), device_id_type=MESH)
    pl.semaphore_wait(barrier, 5 + z * (Z - 1 - z) // 2)

    def piece(k, p):
        start = pl.multiple_of(p * shard_rows + (k % HALVES) * piece_rows, 16)
        return panel.at[k // HALVES, pl.ds(start, piece_rows), :]

    def gather_copy(direction, k, p, own=False):
        if own:
            source = weights[k // HALVES].at[pl.ds((k % HALVES) * piece_rows, piece_rows), :]
        else:
            source = piece(k, p)
        return pltpu.make_async_remote_copy(
            src_ref=source, dst_ref=piece(k, p),
            send_sem=gather_send.at[direction, p, k], recv_sem=gather_recv.at[p, k],
            device_id=targets[direction], device_id_type=MESH,
        )

    def gather_send_piece(direction, k, p, own=False):
        when(direction, lambda: gather_copy(direction, k, p, own).start())

    def gather_wait(k, p):
        gather_copy(ACROSS, k, p).wait_recv()

    mine, facing = dp, z * X + other_x
    for k in range(PIECES):
        for direction in (ACROSS, RIGHT, LEFT):
            gather_send_piece(direction, k, mine, own=True)

    loads = []
    for t in range(3):
        rows = pl.ds(pl.multiple_of(mine * shard_rows, 16), shard_rows)
        loads.append(pltpu.make_async_copy(weights[t], panel.at[t, rows, :], load_sem.at[t]))
    loads.append(pltpu.make_async_copy(tokens_hbm, tokens, load_sem.at[3]))
    loads.append(pltpu.make_async_copy(cotangent_hbm, cotangent, load_sem.at[4]))
    for load in loads:
        load.start()

    slots = lax.broadcasted_iota(jnp.int32, (1, row_count), 1)
    live_gate = jnp.where(slots // BLOCK < count_ref[0], gates_ref[...], 0.0)
    rows_here = lax.broadcasted_iota(jnp.int32, (row_count, 1), 0)
    row_gate[...] = jnp.sum(
        jnp.where(rows_here == routes_ref[...], live_gate, 0.0), axis=1, keepdims=True)
    for acc in (gate_acc, up_acc, back_acc):
        acc[...] = jnp.zeros_like(acc)
    for load in loads:
        load.wait()

    @pl.loop(0, tokens.shape[1] // 128)
    def _(i):
        columns = pl.ds(pl.multiple_of(i * 128, 128), 128)
        flipped[columns, :] = tokens[:, columns].T

    def project(at):
        for k in range(PIECES):
            if k not in X_FIRST:
                gather_wait(k, at * X + other_x)
        span = pl.ds(pl.multiple_of(at * pair_rows, 128), pair_rows)
        for t, (acc, rows) in enumerate(
            ((gate_acc, tokens), (up_acc, tokens), (back_acc, cotangent))
        ):
            acc[...] += jnp.dot(rows[:, span], panel[t, span, :], preferred_element_type=jnp.float32)

    for k in X_FIRST:
        gather_wait(k, facing)
        for direction in (RIGHT, LEFT):
            gather_send_piece(direction, k, facing)

    def arrivals(distance, k):
        for came, onward, exists in (
            (z - distance, RIGHT, z >= distance), (z + distance, LEFT, z + distance < Z)
        ):
            @pl.when(exists)
            def _(came=came, onward=onward):
                gather_wait(k, came * X + x)
                gather_send_piece(onward, k, came * X + x)
                if k in X_FIRST:
                    gather_wait(k, came * X + other_x)
                    gather_send_piece(onward, k, came * X + other_x)
                else:
                    gather_send_piece(ACROSS, k, came * X + x)

    for distance in range(1, Z):
        for k in range(PIECES):
            arrivals(distance, k)
        if distance == 1:
            project(z)
        else:
            pl.when(z >= distance - 1)(lambda: project(z - distance + 1))
            pl.when(z + distance - 1 < Z)(lambda: project(z + distance - 1))
    pl.when(z == Z - 1)(lambda: project(z - (Z - 1)))
    pl.when(z == 0)(lambda: project(z + Z - 1))

    @pl.loop(0, row_count // 64)
    def _(i):
        rows = pl.ds(pl.multiple_of(i * 64, 64), 64)
        gate_val, up_val = gate_acc[rows, :], up_acc[rows, :]
        hidden_grad = row_gate[rows, :] * back_acc[rows, :]
        gate_sigmoid = jax.nn.sigmoid(gate_val)
        grads[1, rows, :] = (hidden_grad * (gate_val * gate_sigmoid)).astype(jnp.bfloat16)
        grads[0, rows, :] = (
            hidden_grad * up_val * gate_sigmoid * (1.0 + gate_val * (1.0 - gate_sigmoid))
        ).astype(jnp.bfloat16)

    def weight_term(at_z, at_x, t):
        start = pl.multiple_of((at_z * X + at_x) * shard_rows, 16)
        return jnp.dot(
            flipped[pl.ds(start, shard_rows), :], grads[t], preferred_element_type=jnp.float32)

    def cross_copy(at, t):
        return pltpu.make_async_remote_copy(
            src_ref=cross_out.at[at, t], dst_ref=cross_in.at[at, t],
            send_sem=cross_send.at[at, t], recv_sem=cross_recv.at[at, t],
            device_id=across, device_id_type=MESH,
        )

    order = (3 * (1 - z // 2), 2 - 2 * z + 5 * (z // 2), 1 + z % 2, z)
    for at in order:
        for t in range(2):
            cross_out[at, t] = weight_term(at, other_x, t).astype(jnp.bfloat16)
            cross_copy(at, t).start()

    def share_copy(j):
        return pltpu.make_async_remote_copy(
            src_ref=share_out.at[j], dst_ref=share_in.at[j],
            send_sem=share_send.at[j], recv_sem=share_recv.at[j],
            device_id=(dp, share_targets[j]), device_id_type=MESH,
        )

    def share_term(to):
        span = pl.ds(pl.multiple_of(to * pair_rows, 16), pair_rows)
        total = None
        for t in range(2):
            term = lax.dot_general(
                grads[t], panel[t, span, :], (((1,), (1,)), ((), ())),
                preferred_element_type=jnp.float32)
            total = term if total is None else total + term
        return total.astype(jnp.bfloat16)

    for j, to in enumerate(share_targets):
        share_out[j] = share_term(to)
        share_copy(j).start()

    @pl.loop(0, Z)
    def _(at):
        for t in range(2):
            own_sum[at, t] = weight_term(at, x, t)

    share_out[Y * C - 1] = share_term(expert)

    sums = {RIGHT: right_sum, LEFT: left_sum}
    upstream = {RIGHT: has[LEFT], LEFT: has[RIGHT]}

    def line_copy(direction, at, t):
        return pltpu.make_async_remote_copy(
            src_ref=sums[direction].at[at, t], dst_ref=sums[direction].at[at, t],
            send_sem=line_send.at[direction, at, t], recv_sem=line_recv.at[direction, at, t],
            device_id=targets[direction], device_id_type=MESH,
        )

    def chunks(fn):
        @pl.loop(0, shard_rows // 64)
        def _(i):
            fn(pl.ds(pl.multiple_of(i * 64, 64), 64))

    def line_step(direction, at):
        for t in range(2):
            cross_copy(at, t).wait_recv()
            def start(rows):
                sums[direction][at, t, rows, :] = (
                    own_sum[at, t, rows, :] + cross_in[at, t, rows, :].astype(jnp.float32)
                ).astype(jnp.bfloat16)
            def add(rows):
                sums[direction][at, t, rows, :] = (
                    own_sum[at, t, rows, :] + cross_in[at, t, rows, :].astype(jnp.float32)
                    + sums[direction][at, t, rows, :].astype(jnp.float32)
                ).astype(jnp.bfloat16)

            @pl.when(upstream[direction])
            def _():
                line_copy(direction, at, t).wait_recv()
                chunks(add)

            @pl.when(jnp.logical_not(upstream[direction]))
            def _():
                chunks(start)

            line_copy(direction, at, t).start()

    for j in range(Z - 1):
        pl.when(z < Z - 1 - j)(lambda: line_step(RIGHT, Z - 1 - j))
        pl.when(z > j)(lambda: line_step(LEFT, j))

    for j in range(Y * C - 1):
        share_copy(j).wait_recv()

    @pl.loop(0, row_count // 64)
    def _(i):
        rows = pl.ds(pl.multiple_of(i * 64, 64), 64)
        total = share_out[Y * C - 1, rows, :].astype(jnp.float32)
        for j in range(Y * C - 1):
            total = total + share_in[j, rows, :].astype(jnp.float32)
        grad_tokens_ref[rows, :] = total.astype(jnp.bfloat16)

    for t, out in enumerate((grad_gate_ref, grad_up_ref)):
        cross_copy(z, t).wait_recv()

        def base(rows):
            own_sum[z, t, rows, :] += cross_in[z, t, rows, :].astype(jnp.float32)
        chunks(base)
        for direction in (RIGHT, LEFT):
            @pl.when(upstream[direction])
            def _():
                line_copy(direction, z, t).wait_recv()
                def add(rows):
                    own_sum[z, t, rows, :] += sums[direction][z, t, rows, :].astype(jnp.float32)
                chunks(add)
        def finish(rows):
            out[rows, :] = own_sum[z, t, rows, :] * scale
        chunks(finish)

    for k in range(PIECES):
        for direction in (ACROSS, RIGHT, LEFT):
            when(direction, lambda: gather_copy(direction, k, mine, own=True).wait_send())
        if k in X_FIRST:
            for direction in (RIGHT, LEFT):
                when(direction, lambda: gather_copy(direction, k, facing).wait_send())
        for distance in range(1, Z):
            for came, onward, exists in (
                (z - distance, RIGHT, z >= distance), (z + distance, LEFT, z + distance < Z)
            ):
                @pl.when(exists)
                def _(came=came, onward=onward):
                    when(onward, lambda: gather_copy(onward, k, came * X + x).wait_send())
                    if k in X_FIRST:
                        when(onward, lambda: gather_copy(onward, k, came * X + other_x).wait_send())
                    else:
                        gather_copy(ACROSS, k, came * X + x).wait_send()
    for t in range(2):
        for at in range(Z):
            cross_copy(at, t).wait_send()
        for at in range(Z):
            pl.when(at > z)(lambda: line_copy(RIGHT, at, t).wait_send())
            pl.when(at < z)(lambda: line_copy(LEFT, at, t).wait_send())
    for j in range(Y * C - 1):
        share_copy(j).wait_send()


def local_kernel(
    tokens, grad_out, route_rows, route_gate, block_count, gate_weight, up_weight, down_weight_t
):
    row_count, features = tokens.shape
    shard_rows, width = gate_weight.shape
    scale = float(lax.axis_size("dp") * row_count) ** (-0.5)
    pair_rows = X * shard_rows
    bf16, f32 = jnp.bfloat16, jnp.float32
    anywhere, vmem = pl.BlockSpec(memory_space=pl.ANY), pl.BlockSpec(memory_space=pltpu.VMEM)
    dma = pltpu.SemaphoreType.DMA
    flops = 2 * row_count * features * width * 7
    return pl.pallas_call(
        functools.partial(kernel, scale),
        out_shape=(
            jax.ShapeDtypeStruct((row_count, pair_rows), bf16),
            jax.ShapeDtypeStruct((shard_rows, width), f32),
            jax.ShapeDtypeStruct((shard_rows, width), f32),
        ),
        in_specs=[
            anywhere, anywhere, vmem, vmem, pl.BlockSpec(memory_space=pltpu.SMEM),
            anywhere, anywhere, anywhere,
        ],
        out_specs=(vmem, vmem, vmem),
        scratch_shapes=[
            pltpu.VMEM((row_count, features), bf16),
            pltpu.VMEM((row_count, features), bf16),
            pltpu.VMEM((3, features, width), bf16),
            pltpu.VMEM((features, row_count), bf16),
            pltpu.VMEM((row_count, width), f32),
            pltpu.VMEM((row_count, width), f32),
            pltpu.VMEM((row_count, width), f32),
            pltpu.VMEM((2, row_count, width), bf16),
            pltpu.VMEM((row_count, 1), f32),
            pltpu.VMEM((Z, 2, shard_rows, width), f32),
            pltpu.VMEM((Z, 2, shard_rows, width), bf16),
            pltpu.VMEM((Z, 2, shard_rows, width), bf16),
            pltpu.VMEM((Z, 2, shard_rows, width), bf16),
            pltpu.VMEM((Z, 2, shard_rows, width), bf16),
            pltpu.VMEM((Y * C, row_count, pair_rows), bf16),
            pltpu.VMEM((Y * C - 1, row_count, pair_rows), bf16),
            dma((5,)),
            dma((3, Z * X, PIECES)), dma((Z * X, PIECES)),
            dma((Z, 2)), dma((Z, 2)),
            dma((2, Z, 2)), dma((2, Z, 2)),
            dma((Y * C - 1,)), dma((Y * C - 1,)),
        ],
        compiler_params=pltpu.CompilerParams(
            collective_id=0, has_side_effects=True, vmem_limit_bytes=62 * 1024 * 1024
        ),
        cost_estimate=pl.CostEstimate(flops=flops, bytes_accessed=16 * 2**20, transcendentals=0),
    )(
        tokens, grad_out, route_rows.reshape(1, -1), route_gate.reshape(1, -1), block_count,
        gate_weight, up_weight, down_weight_t,
    )


def local_plain(
    tokens, grad_out, route_rows, route_gate, block_count, gate_weight, up_weight, down_weight_t
):
    row_count = tokens.shape[0]
    width = gate_weight.shape[1]
    gate_panel, up_panel, down_panel = (
        lax.all_gather(weight, "dp", axis=0, tiled=True)
        for weight in (gate_weight, up_weight, down_weight_t)
    )
    both_panels = jnp.concatenate([gate_panel, up_panel], axis=1)
    live = jnp.arange(row_count) // BLOCK < block_count[0]
    live_gate = jnp.zeros_like(route_gate).at[route_rows].set(jnp.where(live, route_gate, 0.0))
    projected = jnp.dot(tokens, both_panels, preferred_element_type=jnp.float32)
    gate_val, up_val = projected[:, :width], projected[:, width:]
    back = jnp.dot(grad_out, down_panel, preferred_element_type=jnp.float32)
    hidden_grad = live_gate[:, None] * back
    gate_sigmoid = jax.nn.sigmoid(gate_val)
    grad_up = hidden_grad * (gate_val * gate_sigmoid)
    grad_gate = hidden_grad * up_val * gate_sigmoid * (1.0 + gate_val * (1.0 - gate_sigmoid))
    grads = jnp.concatenate([grad_gate, grad_up], axis=1).astype(jnp.bfloat16)
    partial = lax.dot_general(
        grads, both_panels, (((1,), (1,)), ((), ())), preferred_element_type=jnp.float32)
    grad_tokens = lax.psum_scatter(
        partial.astype(jnp.bfloat16), "expert", scatter_dimension=1, tiled=True)
    weight_share = lax.psum_scatter(
        lax.dot_general(
            tokens, grads, (((0,), (0,)), ((), ())), preferred_element_type=jnp.float32),
        "dp", scatter_dimension=0, tiled=True)
    weight_share = weight_share * float(lax.axis_size("dp") * row_count) ** (-0.5)
    return grad_tokens, weight_share[:, :width], weight_share[:, width:]


def solution(mesh):
    by_dp, both = P("dp"), P("dp", "expert")
    in_specs = (P("dp", None), P("dp", None), by_dp, by_dp, by_dp, both, both, both)
    small = (mesh.shape["dp"], mesh.shape["expert"]) == (Z * X, Y * C)
    return jax.shard_map(
        local_kernel if small else local_plain,
        mesh=mesh, in_specs=in_specs, out_specs=(both, both, both), check_vma=False)
```

```python
import functools

import jax
import jax.numpy as jnp
from jax import lax
from jax.experimental import pallas as pl
from jax.experimental.pallas import tpu as pltpu
from jax.sharding import PartitionSpec as P

BLOCK = 128
MESH = pl.DeviceIdType.MESH
Z, X, Y, C = 4, 2, 2, 2
HALVES = 2
PIECES = 3 * HALVES
X_FIRST = (0, 3, 4)
RIGHT, LEFT, ACROSS = 0, 1, 2


def kernel(
    scale,
    tokens_hbm, cotangent_hbm, routes_ref, gates_ref, count_ref, gate_hbm, up_hbm, down_hbm,
    grad_tokens_ref, grad_gate_ref, grad_up_ref,
    tokens, cotangent, panel, flipped, gate_acc, up_acc, back_acc, grads, row_gate,
    own_sum, cross_out, cross_in, right_sum, left_sum, share_out, share_in,
    load_sem, gather_send, gather_recv, cross_send, cross_recv,
    line_send, line_recv, share_send, share_recv,
):
    dp, expert = lax.axis_index("dp"), lax.axis_index("expert")
    z, x = dp // X, dp % X
    y, c = expert // C, expert % C
    other_x = 1 - x
    weights = (gate_hbm, up_hbm, down_hbm)
    shard_rows, width = gate_hbm.shape
    half_width = width // HALVES
    pair_rows = X * shard_rows
    row_count = tokens.shape[0]

    across = (z * X + other_x, expert)
    targets = {RIGHT: (dp + X, expert), LEFT: (dp - X, expert), ACROSS: across}
    has = {RIGHT: z < Z - 1, LEFT: z > 0}

    def when(direction, fn):
        if direction == ACROSS:
            fn()
        else:
            pl.when(has[direction])(fn)

    share_targets = []
    for j in range(1, Y * C):
        y_to = 1 - y if j // C else y
        c_to = 1 - c if j % C else c
        share_targets.append(y_to * C + c_to)

    barrier = pltpu.get_barrier_semaphore()
    for direction in (RIGHT, LEFT, ACROSS):
        when(direction, lambda direction=direction: pl.semaphore_signal(
            barrier, inc=1, device_id=targets[direction], device_id_type=MESH))
    for to in share_targets:
        pl.semaphore_signal(barrier, inc=1, device_id=(dp, to), device_id_type=MESH)
    pl.semaphore_wait(barrier, 5 + z * (Z - 1 - z) // 2)

    def piece(k, p):
        start = pl.multiple_of(p * shard_rows, 16)
        return panel.at[k // 3, k % 3, pl.ds(start, shard_rows), :]

    def gather_copy(direction, k, p, own=False):
        if own:
            source = weights[k % 3].at[:, pl.ds(k // 3 * half_width, half_width)]
        else:
            source = piece(k, p)
        return pltpu.make_async_remote_copy(
            src_ref=source, dst_ref=piece(k, p),
            send_sem=gather_send.at[direction, p, k], recv_sem=gather_recv.at[p, k],
            device_id=targets[direction], device_id_type=MESH,
        )

    def gather_send_piece(direction, k, p, own=False):
        when(direction, lambda: gather_copy(direction, k, p, own).start())

    def gather_wait(k, p):
        gather_copy(ACROSS, k, p).wait_recv()

    mine, facing = dp, z * X + other_x
    for k in range(3):
        for direction in (ACROSS, RIGHT, LEFT):
            gather_send_piece(direction, k, mine, own=True)

    loads = []
    for k in range(PIECES):
        columns = pl.ds(k // 3 * half_width, half_width)
        loads.append(pltpu.make_async_copy(
            weights[k % 3].at[:, columns], piece(k, mine), load_sem.at[k]))
    loads.append(pltpu.make_async_copy(tokens_hbm, tokens, load_sem.at[PIECES]))
    loads.append(pltpu.make_async_copy(cotangent_hbm, cotangent, load_sem.at[PIECES + 1]))
    for load in loads:
        load.start()

    slots = lax.broadcasted_iota(jnp.int32, (1, row_count), 1)
    live_gate = jnp.where(slots // BLOCK < count_ref[0], gates_ref[...], 0.0)
    rows_here = lax.broadcasted_iota(jnp.int32, (row_count, 1), 0)
    row_gate[...] = jnp.sum(
        jnp.where(rows_here == routes_ref[...], live_gate, 0.0), axis=1, keepdims=True)
    for load in loads:
        load.wait()

    @pl.loop(0, tokens.shape[1] // 128)
    def _(i):
        columns = pl.ds(pl.multiple_of(i * 128, 128), 128)
        flipped[columns, :] = tokens[:, columns].T

    def project(at, half):
        for k in range(half * 3, half * 3 + 3):
            if k not in X_FIRST:
                gather_wait(k, at * X + other_x)
        span = pl.ds(pl.multiple_of(at * pair_rows, 128), pair_rows)
        for t, (acc, rows) in enumerate(
            ((gate_acc, tokens), (up_acc, tokens), (back_acc, cotangent))
        ):
            acc[...] += jnp.dot(
                rows[:, span], panel[half, t, span, :], preferred_element_type=jnp.float32)

    def pass_facing(k):
        gather_wait(k, facing)
        for direction in (RIGHT, LEFT):
            gather_send_piece(direction, k, facing)

    def arrivals(distance, k):
        for came, onward, exists in (
            (z - distance, RIGHT, z >= distance), (z + distance, LEFT, z + distance < Z)
        ):
            @pl.when(exists)
            def _(came=came, onward=onward):
                gather_wait(k, came * X + x)
                gather_send_piece(onward, k, came * X + x)
                if k in X_FIRST:
                    gather_wait(k, came * X + other_x)
                    gather_send_piece(onward, k, came * X + other_x)
                else:
                    gather_send_piece(ACROSS, k, came * X + x)

    def hidden_gradients(half):
        @pl.loop(0, row_count // 64)
        def _(i):
            rows = pl.ds(pl.multiple_of(i * 64, 64), 64)
            gate_val, up_val = gate_acc[rows, :], up_acc[rows, :]
            hidden_grad = row_gate[rows, :] * back_acc[rows, :]
            gate_sigmoid = jax.nn.sigmoid(gate_val)
            grads[half, rows, half_width:] = (
                hidden_grad * (gate_val * gate_sigmoid)).astype(jnp.bfloat16)
            grads[half, rows, :half_width] = (
                hidden_grad * up_val * gate_sigmoid * (1.0 + gate_val * (1.0 - gate_sigmoid))
            ).astype(jnp.bfloat16)

    def weight_term(at_z, at_x, t):
        start = pl.multiple_of((at_z * X + at_x) * shard_rows, 16)
        return jnp.dot(
            flipped[pl.ds(start, shard_rows), :], grads[t], preferred_element_type=jnp.float32)

    def cross_copy(at, t):
        return pltpu.make_async_remote_copy(
            src_ref=cross_out.at[at, t], dst_ref=cross_in.at[at, t],
            send_sem=cross_send.at[at, t], recv_sem=cross_recv.at[at, t],
            device_id=across, device_id_type=MESH,
        )

    order = (3 * (1 - z // 2), 2 - 2 * z + 5 * (z // 2), 1 + z % 2, z)
    def send_terms(t):
        for at in order:
            cross_out[at, t] = weight_term(at, other_x, t).astype(jnp.bfloat16)
            cross_copy(at, t).start()

    def keep_terms(t):
        @pl.loop(0, Z)
        def _(at):
            own_sum[at, t] = weight_term(at, x, t)

    def share_copy(j):
        return pltpu.make_async_remote_copy(
            src_ref=share_out.at[j], dst_ref=share_in.at[j],
            send_sem=share_send.at[j], recv_sem=share_recv.at[j],
            device_id=(dp, share_targets[j]), device_id_type=MESH,
        )

    def share_term(to):
        span = pl.ds(pl.multiple_of(to * pair_rows, 16), pair_rows)
        total = None
        for half in range(HALVES):
            for t in range(2):
                term = lax.dot_general(
                    grads[half, :, t * half_width:(t + 1) * half_width], panel[half, t, span, :],
                    (((1,), (1,)), ((), ())), preferred_element_type=jnp.float32)
                total = term if total is None else total + term
        return total.astype(jnp.bfloat16)

    sums = {RIGHT: right_sum, LEFT: left_sum}
    upstream = {RIGHT: has[LEFT], LEFT: has[RIGHT]}

    def line_copy(direction, at, t):
        return pltpu.make_async_remote_copy(
            src_ref=sums[direction].at[at, t], dst_ref=sums[direction].at[at, t],
            send_sem=line_send.at[direction, at, t], recv_sem=line_recv.at[direction, at, t],
            device_id=targets[direction], device_id_type=MESH,
        )

    def chunks(fn):
        @pl.loop(0, shard_rows // 64)
        def _(i):
            fn(pl.ds(pl.multiple_of(i * 64, 64), 64))

    def line_step(direction, at, t):
        cross_copy(at, t).wait_recv()

        def start(rows):
            sums[direction][at, t, rows, :] = (
                own_sum[at, t, rows, :] + cross_in[at, t, rows, :].astype(jnp.float32)
            ).astype(jnp.bfloat16)

        def add(rows):
            sums[direction][at, t, rows, :] = (
                own_sum[at, t, rows, :] + cross_in[at, t, rows, :].astype(jnp.float32)
                + sums[direction][at, t, rows, :].astype(jnp.float32)
            ).astype(jnp.bfloat16)

        @pl.when(upstream[direction])
        def _():
            line_copy(direction, at, t).wait_recv()
            chunks(add)

        @pl.when(jnp.logical_not(upstream[direction]))
        def _():
            chunks(start)

        line_copy(direction, at, t).start()

    def line_round(j, t):
        pl.when(z < Z - 1 - j)(lambda: line_step(RIGHT, Z - 1 - j, t))
        pl.when(z > j)(lambda: line_step(LEFT, j, t))

    for half in range(HALVES):
        pieces = range(half * 3, half * 3 + 3)
        for acc in (gate_acc, up_acc, back_acc):
            acc[...] = jnp.zeros_like(acc)
        if half == 0:
            pass_facing(0)
        for distance in range(1, Z):
            for k in pieces:
                arrivals(distance, k)
            if half == 0 and distance == 2:
                for k in range(3, PIECES):
                    for direction in (ACROSS, RIGHT, LEFT):
                        if k in X_FIRST or direction != ACROSS:
                            gather_send_piece(direction, k, mine, own=True)
            if half == 0 and distance == 3:
                for k in range(3, PIECES):
                    if k in X_FIRST:
                        pass_facing(k)
                    else:
                        gather_send_piece(ACROSS, k, mine, own=True)
            if distance == 1:
                project(z, half)
            else:
                pl.when(z >= distance - 1)(lambda: project(z - distance + 1, half))
                pl.when(z + distance - 1 < Z)(lambda: project(z + distance - 1, half))
            if half == 1:
                line_round(distance - 1, 0)
        pl.when(z == Z - 1)(lambda: project(z - (Z - 1), half))
        pl.when(z == 0)(lambda: project(z + Z - 1, half))
        hidden_gradients(half)
        send_terms(half)
        if half == 1:
            for j, to in enumerate(share_targets):
                share_out[j] = share_term(to)
                share_copy(j).start()
        keep_terms(half)

    share_out[Y * C - 1] = share_term(expert)
    for j in range(Z - 1):
        line_round(j, 1)

    for j in range(Y * C - 1):
        share_copy(j).wait_recv()

    @pl.loop(0, row_count // 64)
    def _(i):
        rows = pl.ds(pl.multiple_of(i * 64, 64), 64)
        total = share_out[Y * C - 1, rows, :].astype(jnp.float32)
        for j in range(Y * C - 1):
            total = total + share_in[j, rows, :].astype(jnp.float32)
        grad_tokens_ref[rows, :] = total.astype(jnp.bfloat16)

    for t in range(HALVES):
        cross_copy(z, t).wait_recv()

        def base(rows):
            own_sum[z, t, rows, :] += cross_in[z, t, rows, :].astype(jnp.float32)
        chunks(base)
        for direction in (RIGHT, LEFT):
            @pl.when(upstream[direction])
            def _():
                line_copy(direction, z, t).wait_recv()
                def add(rows):
                    own_sum[z, t, rows, :] += sums[direction][z, t, rows, :].astype(jnp.float32)
                chunks(add)
        def finish(rows):
            columns = pl.ds(t * half_width, half_width)
            grad_gate_ref[rows, columns] = own_sum[z, t, rows, :half_width] * scale
            grad_up_ref[rows, columns] = own_sum[z, t, rows, half_width:] * scale
        chunks(finish)

    for k in range(PIECES):
        for direction in (ACROSS, RIGHT, LEFT):
            when(direction, lambda: gather_copy(direction, k, mine, own=True).wait_send())
        if k in X_FIRST:
            for direction in (RIGHT, LEFT):
                when(direction, lambda: gather_copy(direction, k, facing).wait_send())
        for distance in range(1, Z):
            for came, onward, exists in (
                (z - distance, RIGHT, z >= distance), (z + distance, LEFT, z + distance < Z)
            ):
                @pl.when(exists)
                def _(came=came, onward=onward):
                    when(onward, lambda: gather_copy(onward, k, came * X + x).wait_send())
                    if k in X_FIRST:
                        when(onward, lambda: gather_copy(onward, k, came * X + other_x).wait_send())
                    else:
                        gather_copy(ACROSS, k, came * X + x).wait_send()
    for t in range(2):
        for at in range(Z):
            cross_copy(at, t).wait_send()
        for at in range(Z):
            pl.when(at > z)(lambda: line_copy(RIGHT, at, t).wait_send())
            pl.when(at < z)(lambda: line_copy(LEFT, at, t).wait_send())
    for j in range(Y * C - 1):
        share_copy(j).wait_send()


def local_kernel(
    tokens, grad_out, route_rows, route_gate, block_count, gate_weight, up_weight, down_weight_t
):
    row_count, features = tokens.shape
    shard_rows, width = gate_weight.shape
    scale = float(lax.axis_size("dp") * row_count) ** (-0.5)
    pair_rows = X * shard_rows
    bf16, f32 = jnp.bfloat16, jnp.float32
    anywhere, vmem = pl.BlockSpec(memory_space=pl.ANY), pl.BlockSpec(memory_space=pltpu.VMEM)
    dma = pltpu.SemaphoreType.DMA
    flops = 2 * row_count * features * width * 7
    return pl.pallas_call(
        functools.partial(kernel, scale),
        out_shape=(
            jax.ShapeDtypeStruct((row_count, pair_rows), bf16),
            jax.ShapeDtypeStruct((shard_rows, width), f32),
            jax.ShapeDtypeStruct((shard_rows, width), f32),
        ),
        in_specs=[
            anywhere, anywhere, vmem, vmem, pl.BlockSpec(memory_space=pltpu.SMEM),
            anywhere, anywhere, anywhere,
        ],
        out_specs=(vmem, vmem, vmem),
        scratch_shapes=[
            pltpu.VMEM((row_count, features), bf16),
            pltpu.VMEM((row_count, features), bf16),
            pltpu.VMEM((HALVES, 3, features, width // HALVES), bf16),
            pltpu.VMEM((features, row_count), bf16),
            pltpu.VMEM((row_count, width // HALVES), f32),
            pltpu.VMEM((row_count, width // HALVES), f32),
            pltpu.VMEM((row_count, width // HALVES), f32),
            pltpu.VMEM((2, row_count, width), bf16),
            pltpu.VMEM((row_count, 1), f32),
            pltpu.VMEM((Z, 2, shard_rows, width), f32),
            pltpu.VMEM((Z, 2, shard_rows, width), bf16),
            pltpu.VMEM((Z, 2, shard_rows, width), bf16),
            pltpu.VMEM((Z, 2, shard_rows, width), bf16),
            pltpu.VMEM((Z, 2, shard_rows, width), bf16),
            pltpu.VMEM((Y * C, row_count, pair_rows), bf16),
            pltpu.VMEM((Y * C - 1, row_count, pair_rows), bf16),
            dma((PIECES + 2,)),
            dma((3, Z * X, PIECES)), dma((Z * X, PIECES)),
            dma((Z, 2)), dma((Z, 2)),
            dma((2, Z, 2)), dma((2, Z, 2)),
            dma((Y * C - 1,)), dma((Y * C - 1,)),
        ],
        compiler_params=pltpu.CompilerParams(
            collective_id=0, has_side_effects=True, vmem_limit_bytes=62 * 1024 * 1024
        ),
        cost_estimate=pl.CostEstimate(flops=flops, bytes_accessed=16 * 2**20, transcendentals=0),
    )(
        tokens, grad_out, route_rows.reshape(1, -1), route_gate.reshape(1, -1), block_count,
        gate_weight, up_weight, down_weight_t,
    )


def local_plain(
    tokens, grad_out, route_rows, route_gate, block_count, gate_weight, up_weight, down_weight_t
):
    row_count = tokens.shape[0]
    width = gate_weight.shape[1]
    gate_panel, up_panel, down_panel = (
        lax.all_gather(weight, "dp", axis=0, tiled=True)
        for weight in (gate_weight, up_weight, down_weight_t)
    )
    both_panels = jnp.concatenate([gate_panel, up_panel], axis=1)
    live = jnp.arange(row_count) // BLOCK < block_count[0]
    live_gate = jnp.zeros_like(route_gate).at[route_rows].set(jnp.where(live, route_gate, 0.0))
    projected = jnp.dot(tokens, both_panels, preferred_element_type=jnp.float32)
    gate_val, up_val = projected[:, :width], projected[:, width:]
    back = jnp.dot(grad_out, down_panel, preferred_element_type=jnp.float32)
    hidden_grad = live_gate[:, None] * back
    gate_sigmoid = jax.nn.sigmoid(gate_val)
    grad_up = hidden_grad * (gate_val * gate_sigmoid)
    grad_gate = hidden_grad * up_val * gate_sigmoid * (1.0 + gate_val * (1.0 - gate_sigmoid))
    grads = jnp.concatenate([grad_gate, grad_up], axis=1).astype(jnp.bfloat16)
    partial = lax.dot_general(
        grads, both_panels, (((1,), (1,)), ((), ())), preferred_element_type=jnp.float32)
    grad_tokens = lax.psum_scatter(
        partial.astype(jnp.bfloat16), "expert", scatter_dimension=1, tiled=True)
    weight_share = lax.psum_scatter(
        lax.dot_general(
            tokens, grads, (((0,), (0,)), ((), ())), preferred_element_type=jnp.float32),
        "dp", scatter_dimension=0, tiled=True)
    weight_share = weight_share * float(lax.axis_size("dp") * row_count) ** (-0.5)
    return grad_tokens, weight_share[:, :width], weight_share[:, width:]


def solution(mesh):
    by_dp, both = P("dp"), P("dp", "expert")
    in_specs = (P("dp", None), P("dp", None), by_dp, by_dp, by_dp, both, both, both)
    small = (mesh.shape["dp"], mesh.shape["expert"]) == (Z * X, Y * C)
    return jax.shard_map(
        local_kernel if small else local_plain,
        mesh=mesh, in_specs=in_specs, out_specs=(both, both, both), check_vma=False)
```

```python
import functools

import jax
import jax.numpy as jnp
from jax import lax
from jax.experimental import pallas as pl
from jax.experimental.pallas import tpu as pltpu
from jax.sharding import PartitionSpec as P

BLOCK = 128
MESH = pl.DeviceIdType.MESH
Z, X, Y, C = 4, 2, 2, 2
HALVES = 2
PIECES = 3 * HALVES
X_FIRST = (0, 3)
RIGHT, LEFT, ACROSS = 0, 1, 2


def kernel(
    scale,
    tokens_hbm, cotangent_hbm, routes_ref, gates_ref, count_ref, gate_hbm, up_hbm, down_hbm,
    grad_tokens_ref, grad_gate_ref, grad_up_ref,
    tokens, cotangent, panel, flipped, gate_acc, up_acc, back_acc, grads, row_gate,
    own_sum, cross_out, cross_in, right_sum, left_sum, share_out, share_in,
    load_sem, gather_send, gather_recv, cross_send, cross_recv,
    line_send, line_recv, share_send, share_recv,
):
    dp, expert = lax.axis_index("dp"), lax.axis_index("expert")
    z, x = dp // X, dp % X
    y, c = expert // C, expert % C
    other_x = 1 - x
    weights = (gate_hbm, up_hbm, down_hbm)
    shard_rows, width = gate_hbm.shape
    half_width = width // HALVES
    pair_rows = X * shard_rows
    row_count = tokens.shape[0]

    across = (z * X + other_x, expert)
    targets = {RIGHT: (dp + X, expert), LEFT: (dp - X, expert), ACROSS: across}
    has = {RIGHT: z < Z - 1, LEFT: z > 0}

    def when(direction, fn):
        if direction == ACROSS:
            fn()
        else:
            pl.when(has[direction])(fn)

    share_targets = []
    for j in range(1, Y * C):
        y_to = 1 - y if j // C else y
        c_to = 1 - c if j % C else c
        share_targets.append(y_to * C + c_to)

    barrier = pltpu.get_barrier_semaphore()
    for direction in (RIGHT, LEFT, ACROSS):
        when(direction, lambda direction=direction: pl.semaphore_signal(
            barrier, inc=1, device_id=targets[direction], device_id_type=MESH))
    for to in share_targets:
        pl.semaphore_signal(barrier, inc=1, device_id=(dp, to), device_id_type=MESH)
    pl.semaphore_wait(barrier, 5 + z * (Z - 1 - z) // 2)

    def piece(k, p):
        start = pl.multiple_of(p * shard_rows, 16)
        return panel.at[k // 3, k % 3, pl.ds(start, shard_rows), :]

    def gather_copy(direction, k, p, own=False):
        if own:
            source = weights[k % 3].at[:, pl.ds(k // 3 * half_width, half_width)]
        else:
            source = piece(k, p)
        return pltpu.make_async_remote_copy(
            src_ref=source, dst_ref=piece(k, p),
            send_sem=gather_send.at[direction, p, k], recv_sem=gather_recv.at[p, k],
            device_id=targets[direction], device_id_type=MESH,
        )

    def gather_send_piece(direction, k, p, own=False):
        when(direction, lambda: gather_copy(direction, k, p, own).start())

    def gather_wait(k, p):
        gather_copy(ACROSS, k, p).wait_recv()

    mine, facing = dp, z * X + other_x
    for k in range(3):
        for direction in (ACROSS, RIGHT, LEFT):
            gather_send_piece(direction, k, mine, own=True)

    loads = []
    for k in range(PIECES):
        columns = pl.ds(k // 3 * half_width, half_width)
        loads.append(pltpu.make_async_copy(
            weights[k % 3].at[:, columns], piece(k, mine), load_sem.at[k]))
    loads.append(pltpu.make_async_copy(tokens_hbm, tokens, load_sem.at[PIECES]))
    loads.append(pltpu.make_async_copy(cotangent_hbm, cotangent, load_sem.at[PIECES + 1]))
    for load in loads:
        load.start()

    slots = lax.broadcasted_iota(jnp.int32, (1, row_count), 1)
    live_gate = jnp.where(slots // BLOCK < count_ref[0], gates_ref[...], 0.0)
    rows_here = lax.broadcasted_iota(jnp.int32, (row_count, 1), 0)
    row_gate[...] = jnp.sum(
        jnp.where(rows_here == routes_ref[...], live_gate, 0.0), axis=1, keepdims=True)
    for load in loads:
        load.wait()

    @pl.loop(0, tokens.shape[1] // 128)
    def _(i):
        columns = pl.ds(pl.multiple_of(i * 128, 128), 128)
        flipped[columns, :] = tokens[:, columns].T

    def project(at, half):
        for k in range(half * 3, half * 3 + 3):
            if k not in X_FIRST:
                gather_wait(k, at * X + other_x)
        span = pl.ds(pl.multiple_of(at * pair_rows, 128), pair_rows)
        for t, (acc, rows) in enumerate(
            ((gate_acc, tokens), (up_acc, tokens), (back_acc, cotangent))
        ):
            acc[...] += jnp.dot(
                rows[:, span], panel[half, t, span, :], preferred_element_type=jnp.float32)

    def pass_facing(k):
        gather_wait(k, facing)
        for direction in (RIGHT, LEFT):
            gather_send_piece(direction, k, facing)

    def arrivals(distance, k):
        for came, onward, exists in (
            (z - distance, RIGHT, z >= distance), (z + distance, LEFT, z + distance < Z)
        ):
            @pl.when(exists)
            def _(came=came, onward=onward):
                gather_wait(k, came * X + x)
                gather_send_piece(onward, k, came * X + x)
                if k in X_FIRST:
                    gather_wait(k, came * X + other_x)
                    gather_send_piece(onward, k, came * X + other_x)
                else:
                    gather_send_piece(ACROSS, k, came * X + x)

    def hidden_gradients(half):
        @pl.loop(0, row_count // 64)
        def _(i):
            rows = pl.ds(pl.multiple_of(i * 64, 64), 64)
            gate_val, up_val = gate_acc[rows, :], up_acc[rows, :]
            hidden_grad = row_gate[rows, :] * back_acc[rows, :]
            gate_sigmoid = jax.nn.sigmoid(gate_val)
            grads[half, rows, half_width:] = (
                hidden_grad * (gate_val * gate_sigmoid)).astype(jnp.bfloat16)
            grads[half, rows, :half_width] = (
                hidden_grad * up_val * gate_sigmoid * (1.0 + gate_val * (1.0 - gate_sigmoid))
            ).astype(jnp.bfloat16)

    def weight_term(at_z, at_x, t):
        start = pl.multiple_of((at_z * X + at_x) * shard_rows, 16)
        return jnp.dot(
            flipped[pl.ds(start, shard_rows), :], grads[t], preferred_element_type=jnp.float32)

    def cross_copy(at, t):
        return pltpu.make_async_remote_copy(
            src_ref=cross_out.at[at, t], dst_ref=cross_in.at[at, t],
            send_sem=cross_send.at[at, t], recv_sem=cross_recv.at[at, t],
            device_id=across, device_id_type=MESH,
        )

    order = (3 * (1 - z // 2), 2 - 2 * z + 5 * (z // 2), 1 + z % 2, z)
    def send_terms(t):
        for at in order:
            cross_out[at, t] = weight_term(at, other_x, t).astype(jnp.bfloat16)
            cross_copy(at, t).start()

    def keep_terms(t):
        @pl.loop(0, Z)
        def _(at):
            own_sum[at, t] = weight_term(at, x, t)

    def share_copy(j):
        return pltpu.make_async_remote_copy(
            src_ref=share_out.at[j], dst_ref=share_in.at[j],
            send_sem=share_send.at[j], recv_sem=share_recv.at[j],
            device_id=(dp, share_targets[j]), device_id_type=MESH,
        )

    def share_term(to):
        span = pl.ds(pl.multiple_of(to * pair_rows, 16), pair_rows)
        total = None
        for half in range(HALVES):
            for t in range(2):
                term = lax.dot_general(
                    grads[half, :, t * half_width:(t + 1) * half_width], panel[half, t, span, :],
                    (((1,), (1,)), ((), ())), preferred_element_type=jnp.float32)
                total = term if total is None else total + term
        return total.astype(jnp.bfloat16)

    sums = {RIGHT: right_sum, LEFT: left_sum}
    upstream = {RIGHT: has[LEFT], LEFT: has[RIGHT]}

    def line_copy(direction, at, t):
        return pltpu.make_async_remote_copy(
            src_ref=sums[direction].at[at, t], dst_ref=sums[direction].at[at, t],
            send_sem=line_send.at[direction, at, t], recv_sem=line_recv.at[direction, at, t],
            device_id=targets[direction], device_id_type=MESH,
        )

    def chunks(fn):
        @pl.loop(0, shard_rows // 64)
        def _(i):
            fn(pl.ds(pl.multiple_of(i * 64, 64), 64))

    def line_step(direction, at, t):
        cross_copy(at, t).wait_recv()

        def start(rows):
            sums[direction][at, t, rows, :] = (
                own_sum[at, t, rows, :] + cross_in[at, t, rows, :].astype(jnp.float32)
            ).astype(jnp.bfloat16)

        def add(rows):
            sums[direction][at, t, rows, :] = (
                own_sum[at, t, rows, :] + cross_in[at, t, rows, :].astype(jnp.float32)
                + sums[direction][at, t, rows, :].astype(jnp.float32)
            ).astype(jnp.bfloat16)

        @pl.when(upstream[direction])
        def _():
            line_copy(direction, at, t).wait_recv()
            chunks(add)

        @pl.when(jnp.logical_not(upstream[direction]))
        def _():
            chunks(start)

        line_copy(direction, at, t).start()

    def line_round(j, t):
        pl.when(z < Z - 1 - j)(lambda: line_step(RIGHT, Z - 1 - j, t))
        pl.when(z > j)(lambda: line_step(LEFT, j, t))

    for half in range(HALVES):
        pieces = range(half * 3, half * 3 + 3)
        for acc in (gate_acc, up_acc, back_acc):
            acc[...] = jnp.zeros_like(acc)
        if half == 0:
            pass_facing(0)
        for distance in range(1, Z):
            for k in pieces:
                arrivals(distance, k)
            if half == 0 and distance == 2:
                for k in range(3, PIECES):
                    for direction in (ACROSS, RIGHT, LEFT):
                        if k in X_FIRST or direction != ACROSS:
                            gather_send_piece(direction, k, mine, own=True)
            if half == 0 and distance == 3:
                for k in range(3, PIECES):
                    if k in X_FIRST:
                        pass_facing(k)
                    else:
                        gather_send_piece(ACROSS, k, mine, own=True)
            if distance == 1:
                project(z, half)
            else:
                pl.when(z >= distance - 1)(lambda: project(z - distance + 1, half))
                pl.when(z + distance - 1 < Z)(lambda: project(z + distance - 1, half))
            if half == 1 and distance == 1:
                keep_terms(0)
            if half == 1 and distance == 2:
                line_round(0, 0)
            if half == 1 and distance == 3:
                line_round(1, 0)
        pl.when(z == Z - 1)(lambda: project(z - (Z - 1), half))
        pl.when(z == 0)(lambda: project(z + Z - 1, half))
        hidden_gradients(half)
        send_terms(half)
        if half == 1:
            for j, to in enumerate(share_targets):
                share_out[j] = share_term(to)
                share_copy(j).start()
            line_round(2, 0)
            keep_terms(1)

    share_out[Y * C - 1] = share_term(expert)
    for j in range(Z - 1):
        line_round(j, 1)

    for j in range(Y * C - 1):
        share_copy(j).wait_recv()

    @pl.loop(0, row_count // 64)
    def _(i):
        rows = pl.ds(pl.multiple_of(i * 64, 64), 64)
        total = share_out[Y * C - 1, rows, :].astype(jnp.float32)
        for j in range(Y * C - 1):
            total = total + share_in[j, rows, :].astype(jnp.float32)
        grad_tokens_ref[rows, :] = total.astype(jnp.bfloat16)

    for t in range(HALVES):
        cross_copy(z, t).wait_recv()

        def base(rows):
            own_sum[z, t, rows, :] += cross_in[z, t, rows, :].astype(jnp.float32)
        chunks(base)
        for direction in (RIGHT, LEFT):
            @pl.when(upstream[direction])
            def _():
                line_copy(direction, z, t).wait_recv()
                def add(rows):
                    own_sum[z, t, rows, :] += sums[direction][z, t, rows, :].astype(jnp.float32)
                chunks(add)
        def finish(rows):
            columns = pl.ds(t * half_width, half_width)
            grad_gate_ref[rows, columns] = own_sum[z, t, rows, :half_width] * scale
            grad_up_ref[rows, columns] = own_sum[z, t, rows, half_width:] * scale
        chunks(finish)

    for k in range(PIECES):
        for direction in (ACROSS, RIGHT, LEFT):
            when(direction, lambda: gather_copy(direction, k, mine, own=True).wait_send())
        if k in X_FIRST:
            for direction in (RIGHT, LEFT):
                when(direction, lambda: gather_copy(direction, k, facing).wait_send())
        for distance in range(1, Z):
            for came, onward, exists in (
                (z - distance, RIGHT, z >= distance), (z + distance, LEFT, z + distance < Z)
            ):
                @pl.when(exists)
                def _(came=came, onward=onward):
                    when(onward, lambda: gather_copy(onward, k, came * X + x).wait_send())
                    if k in X_FIRST:
                        when(onward, lambda: gather_copy(onward, k, came * X + other_x).wait_send())
                    else:
                        gather_copy(ACROSS, k, came * X + x).wait_send()
    for t in range(2):
        for at in range(Z):
            cross_copy(at, t).wait_send()
        for at in range(Z):
            pl.when(at > z)(lambda: line_copy(RIGHT, at, t).wait_send())
            pl.when(at < z)(lambda: line_copy(LEFT, at, t).wait_send())
    for j in range(Y * C - 1):
        share_copy(j).wait_send()


def local_kernel(
    tokens, grad_out, route_rows, route_gate, block_count, gate_weight, up_weight, down_weight_t
):
    row_count, features = tokens.shape
    shard_rows, width = gate_weight.shape
    scale = float(lax.axis_size("dp") * row_count) ** (-0.5)
    pair_rows = X * shard_rows
    bf16, f32 = jnp.bfloat16, jnp.float32
    anywhere, vmem = pl.BlockSpec(memory_space=pl.ANY), pl.BlockSpec(memory_space=pltpu.VMEM)
    dma = pltpu.SemaphoreType.DMA
    flops = 2 * row_count * features * width * 7
    return pl.pallas_call(
        functools.partial(kernel, scale),
        out_shape=(
            jax.ShapeDtypeStruct((row_count, pair_rows), bf16),
            jax.ShapeDtypeStruct((shard_rows, width), f32),
            jax.ShapeDtypeStruct((shard_rows, width), f32),
        ),
        in_specs=[
            anywhere, anywhere, vmem, vmem, pl.BlockSpec(memory_space=pltpu.SMEM),
            anywhere, anywhere, anywhere,
        ],
        out_specs=(vmem, vmem, vmem),
        scratch_shapes=[
            pltpu.VMEM((row_count, features), bf16),
            pltpu.VMEM((row_count, features), bf16),
            pltpu.VMEM((HALVES, 3, features, width // HALVES), bf16),
            pltpu.VMEM((features, row_count), bf16),
            pltpu.VMEM((row_count, width // HALVES), f32),
            pltpu.VMEM((row_count, width // HALVES), f32),
            pltpu.VMEM((row_count, width // HALVES), f32),
            pltpu.VMEM((2, row_count, width), bf16),
            pltpu.VMEM((row_count, 1), f32),
            pltpu.VMEM((Z, 2, shard_rows, width), f32),
            pltpu.VMEM((Z, 2, shard_rows, width), bf16),
            pltpu.VMEM((Z, 2, shard_rows, width), bf16),
            pltpu.VMEM((Z, 2, shard_rows, width), bf16),
            pltpu.VMEM((Z, 2, shard_rows, width), bf16),
            pltpu.VMEM((Y * C, row_count, pair_rows), bf16),
            pltpu.VMEM((Y * C - 1, row_count, pair_rows), bf16),
            dma((PIECES + 2,)),
            dma((3, Z * X, PIECES)), dma((Z * X, PIECES)),
            dma((Z, 2)), dma((Z, 2)),
            dma((2, Z, 2)), dma((2, Z, 2)),
            dma((Y * C - 1,)), dma((Y * C - 1,)),
        ],
        compiler_params=pltpu.CompilerParams(
            collective_id=0, has_side_effects=True, vmem_limit_bytes=62 * 1024 * 1024
        ),
        cost_estimate=pl.CostEstimate(flops=flops, bytes_accessed=16 * 2**20, transcendentals=0),
    )(
        tokens, grad_out, route_rows.reshape(1, -1), route_gate.reshape(1, -1), block_count,
        gate_weight, up_weight, down_weight_t,
    )


def local_plain(
    tokens, grad_out, route_rows, route_gate, block_count, gate_weight, up_weight, down_weight_t
):
    row_count = tokens.shape[0]
    width = gate_weight.shape[1]
    gate_panel, up_panel, down_panel = (
        lax.all_gather(weight, "dp", axis=0, tiled=True)
        for weight in (gate_weight, up_weight, down_weight_t)
    )
    both_panels = jnp.concatenate([gate_panel, up_panel], axis=1)
    live = jnp.arange(row_count) // BLOCK < block_count[0]
    live_gate = jnp.zeros_like(route_gate).at[route_rows].set(jnp.where(live, route_gate, 0.0))
    projected = jnp.dot(tokens, both_panels, preferred_element_type=jnp.float32)
    gate_val, up_val = projected[:, :width], projected[:, width:]
    back = jnp.dot(grad_out, down_panel, preferred_element_type=jnp.float32)
    hidden_grad = live_gate[:, None] * back
    gate_sigmoid = jax.nn.sigmoid(gate_val)
    grad_up = hidden_grad * (gate_val * gate_sigmoid)
    grad_gate = hidden_grad * up_val * gate_sigmoid * (1.0 + gate_val * (1.0 - gate_sigmoid))
    grads = jnp.concatenate([grad_gate, grad_up], axis=1).astype(jnp.bfloat16)
    partial = lax.dot_general(
        grads, both_panels, (((1,), (1,)), ((), ())), preferred_element_type=jnp.float32)
    grad_tokens = lax.psum_scatter(
        partial.astype(jnp.bfloat16), "expert", scatter_dimension=1, tiled=True)
    weight_share = lax.psum_scatter(
        lax.dot_general(
            tokens, grads, (((0,), (0,)), ((), ())), preferred_element_type=jnp.float32),
        "dp", scatter_dimension=0, tiled=True)
    weight_share = weight_share * float(lax.axis_size("dp") * row_count) ** (-0.5)
    return grad_tokens, weight_share[:, :width], weight_share[:, width:]


def solution(mesh):
    by_dp, both = P("dp"), P("dp", "expert")
    in_specs = (P("dp", None), P("dp", None), by_dp, by_dp, by_dp, both, both, both)
    small = (mesh.shape["dp"], mesh.shape["expert"]) == (Z * X, Y * C)
    return jax.shard_map(
        local_kernel if small else local_plain,
        mesh=mesh, in_specs=in_specs, out_specs=(both, both, both), check_vma=False)
```
